128 devices in a mesh: dp: 8 (over z, core), rank: 16 (over x, y).
Axes of the slice: x: 4, y: 4, z: 4, core: 2. Of those that a mesh axis runs over, the one named last changes fastest.
Arguments:
- acts: bfloat16 [384, 256, 4096], P('dp', None, 'rank'), may hold values from -6 to 6
- grads: bfloat16 [384, 256, 11008], P('dp', None, 'rank'), may hold values from -6 to 6
- proj_in: bfloat16 [4096, 64], P('rank'), may hold values from -0.09375 to 0.09375
- proj_out: bfloat16 [11008, 64], P('rank'), may hold values from -0.0546875 to 0.0546875
- queries: float32 [4096, 4096], P('rank'), may hold values from -0.09375 to 0.09375
- seg_emb: int32 [384], P('dp'), may hold values from 0 to 15
- query_emb: int32 [4096], P('rank'), may hold values from 0 to 15
- compat: int32 [16, 16], replicated, may hold values from 0 to 1, as said below
- counts: int32 [384], P('dp'), may hold values from 32 to 256
Outputs:
- influence: float32 [384, 4096], P('dp', 'rank')
The draws below stay inside these ranges and needn't reach their ends.
Inputs may be any that keep to these rules, and one draw needn't show every extreme that they name: compat has ones on its diagonal.
All inputs are finite; a program needn't handle non-finite values.
Results may differ from the reference program's by a relative error of at most 0.0003.
Values sent between devices are 32-bit elements; how exact they have to be, the bound alone decides.
No kernel may reach another device: no remote copies, remote signals or barrier semaphores. Data moves between devices by JAX's collectives and lax.ppermute only.
A program may use at most 128 MiB of HBM per device.

```python
import math
import jax
import jax.numpy as jnp
import numpy as np
from jax import lax

DIN = 4096
DOUT = 11008
FACTOR = 64
TOK = 256
EMB = 16
SEGMENTS = 384
QUERIES = 4096


def draw_compat(key, part):
    key = jax.random.fold_in(key, 7)
    random_bits = jax.random.randint(key, (EMB, EMB), 0, 2).astype(jnp.int32)
    rows = lax.broadcasted_iota(jnp.int32, (EMB, EMB), 0)
    cols = lax.broadcasted_iota(jnp.int32, (EMB, EMB), 1)
    return jnp.maximum(random_bits, (rows == cols).astype(jnp.int32))


def touch_ends(result, key, low, high):
    extent = result.shape
    index_at = [jax.random.randint(jax.random.fold_in(key, axis), (), 0, extent[axis]) for axis in range(len(extent))]
    result = result.at[tuple(index_at)].set(low)
    longest = extent.index(max(extent))
    index_at[longest] = (index_at[longest] + 1) % extent[longest]
    return result.at[tuple(index_at)].set(high)


def level_of(rng, extent, cuts, least, high):
    def one(position, blocks):
        draws = jax.random.uniform(jax.random.fold_in(jax.random.fold_in(rng, 6), position), (blocks,), jnp.float32, least / len(cuts), high / len(cuts))
        return jnp.repeat(jnp.exp(draws), extent[position] // blocks).reshape((-1,) + (1,) * (len(extent) - position - 1))

    loudness = one(*cuts[0])
    for cut in cuts[1:]:
        loudness = loudness * one(*cut)
    return loudness


def rank_table(amount, slope):
    weights = [(1 << 20) // math.isqrt(standing ** slope) + 1 for standing in range(1, amount + 1)]
    scale = 1 + sum(weights) // (1 << 30)
    return np.cumsum(np.array([max(1, weight // scale) for weight in weights]))


def ranked_ids(own_key, extent, amount, lean):
    listing = rank_table(amount, lean)
    lot = jax.random.randint(jax.random.fold_in(own_key, 1), extent, 0, int(listing[amount - 1]))
    rank = jnp.searchsorted(jnp.asarray(listing, jnp.int32), lot, side="right")
    return jax.random.permutation(jax.random.fold_in(own_key, 2), amount)[rank].astype(jnp.int32)


def normal_values(own_key, shape, width, bound, split=(), held_as=jnp.bfloat16):
    drawn = width * jax.random.normal(own_key, shape, jnp.float32)
    if split:
        drawn = drawn * level_of(own_key, shape, split, -0.22, 0.18)
    return jnp.clip(drawn, -bound, bound).astype(held_as)


def setup_inputs(seed: int = 0) -> dict:
    streams_of = jax.random.split(jax.random.key(seed), 10)
    return {
        "acts": normal_values(streams_of[0], (SEGMENTS, TOK, DIN), 1.0, 6.0, ((0, 8), (2, 16))),
        "grads": normal_values(streams_of[1], (SEGMENTS, TOK, DOUT), 1.0, 6.0, ((0, 8), (2, 16))),
        "proj_in": normal_values(streams_of[2], (DIN, FACTOR), DIN ** -0.5, 0.09375, ((0, 16),)),
        "proj_out": normal_values(streams_of[3], (DOUT, FACTOR), DOUT ** -0.5, 0.0546875, ((0, 16),)),
        "queries": normal_values(streams_of[4], (QUERIES, FACTOR * FACTOR), (FACTOR * FACTOR) ** -0.5, 0.09375, ((0, 16),), jnp.float32),
        "seg_emb": touch_ends(ranked_ids(streams_of[5], (SEGMENTS,), EMB, 2), jax.random.fold_in(streams_of[5], 3), 0, EMB - 1).astype(jnp.int32),
        "query_emb": touch_ends(jax.random.randint(streams_of[6], (QUERIES,), 0, EMB), jax.random.fold_in(streams_of[6], 1), 0, EMB - 1).astype(jnp.int32),
        "compat": draw_compat(jax.random.fold_in(streams_of[9], 71), 0),
        "counts": touch_ends(jax.random.randint(streams_of[8], (SEGMENTS,), TOK // 8, TOK + 1), jax.random.fold_in(streams_of[8], 1), TOK // 8, TOK).astype(jnp.int32),
    }


def reference(acts, grads, proj_in, proj_out, queries, seg_emb, query_emb, compat, counts):

    def feature(items):
        act_rows, grad_rows, live = items
        proj_a = jnp.dot(act_rows, proj_in, preferred_element_type=jnp.float32)
        proj_g = jnp.dot(grad_rows, proj_out, preferred_element_type=jnp.float32)
        keep = (jnp.arange(TOK, dtype=jnp.int32) < live).astype(jnp.float32)[:, None]
        outer = jnp.dot((proj_g * keep).T, proj_a, precision=lax.Precision.HIGHEST)
        return outer.reshape(FACTOR * FACTOR)
    feats = lax.map(feature, (acts, grads, counts))
    raw = jnp.dot(feats, queries.T, precision=lax.Precision.HIGHEST)
    allowed = compat[seg_emb][:, query_emb].astype(jnp.float32)
    raw = raw * allowed
    power = lax.optimization_barrier(jnp.mean(raw * raw, axis=0))
    return raw / jnp.sqrt(power + 1e-06)
```

```python
import functools

import jax
import jax.numpy as jnp
import numpy as np
from jax import lax
from jax.experimental import pallas as pl
from jax.experimental.pallas import tpu as pltpu
from jax.sharding import PartitionSpec as P

SIDE = 4
RANKS = SIDE * SIDE
SLOTS = 3
BF16 = jnp.bfloat16
F32 = jnp.float32
LADDER = (768,)


def at(x, y):
    return (x % SIDE) * SIDE + y % SIDE


def receiver(role, d, rank):
    x, y = divmod(rank, SIDE)
    even = (x + y + d) % 2 == 0
    return at(x + d, y) if even == (role == 1) else at(x, y + d)


def second(kind, rank):
    x, y = divmod(rank, SIDE)
    even = (x + y) % 2 == 0
    if kind == 3:
        return at(x, y + 2) if even else at(x + 2, y)
    step = 1 if kind == 1 else -1
    return at(x + step, y) if even else at(x, y + step)


def destinations(rank):
    order = []
    for d in range(SIDE):
        r1, r2 = receiver(1, d, rank), receiver(2, d, rank)
        order += [r1, second(3, r1), second(1, r2), second(2, r2)]
    return order


def slot_positions(rank):
    zig = 7 - rank // 2 if rank % 2 == 0 else 15 - rank // 2
    sums = [r + (7 - r // 2 if r % 2 == 0 else 15 - r // 2) for r in range(RANKS)]
    above = sum(s > sums[rank] or (s == sums[rank] and r > rank) for r, s in enumerate(sums))
    return [rank, RANKS + zig, 2 * RANKS + above]


def gathered(rank):
    x, y = divmod(rank, SIDE)
    return [at(x - dx, y - dy) for dy in range(SIDE) for dx in range(SIDE)]


PROJECT_POS = np.array([sum((slot_positions(q) for q in destinations(r)), []) for r in range(RANKS)], np.int32)
GATHER_POS = np.array([sum((slot_positions(q) for q in gathered(r)), []) for r in range(RANKS)], np.int32)
OWNER_POS = np.array([slot_positions(q) for q in range(RANKS)], np.int32).T.reshape(-1)
FIRST = {(role, d): [(r, receiver(role, d, r)) for r in range(RANKS)] for role in (1, 2) for d in range(1, SIDE)}
SECOND = {kind: [(r, second(kind, r)) for r in range(RANKS)] for kind in (1, 2, 3)}


def shift(dx, dy):
    return [(r, at(r // SIDE + dx, r % SIDE + dy)) for r in range(RANKS)]


def up(n, m):
    return (n + (m - 1)) // m * m


def project_kernel(part, cap, segs, cnts, *refs):
    acts, grads = refs[0:3], refs[3:6]
    w_in, w_out, out1, out2, spill = refs[6:]
    step = pl.program_id(0)
    toks = acts[0].shape[1]
    w_a = jnp.concatenate([jnp.zeros_like(w_in[...]), w_in[...]], axis=0)
    nt = (((1,), (1,)), ((), ()))

    def rows(k):
        side_a = lax.dot_general(acts[k][0], w_a, nt, preferred_element_type=F32)
        side_g = jnp.dot(w_out[...], grads[k][0], preferred_element_type=F32)
        return side_a + jnp.concatenate([side_g, jnp.zeros_like(side_g)], axis=0).T

    base = part * 12 + step * SLOTS
    off1 = pl.multiple_of(up(cnts[base], 8), 8)
    off2 = pl.multiple_of(off1 + up(cnts[base + 1], 8), 8)
    pieces = up(cnts[base + 2], 16) // 16

    def write(out):
        out[pl.ds(0, toks), :] = rows(0)
        out[pl.ds(off1, toks), :] = rows(1)
        spill[...] = rows(2)

        def piece(i, _):
            to = pl.multiple_of(off2 + i * 16, 8)
            out[pl.ds(to, 16), :] = spill[pl.ds(pl.multiple_of(i * 16, 16), 16), :]
            return 0

        lax.fori_loop(0, pieces, piece, 0)

    pl.when(step < 2)(lambda: write(out1))
    pl.when(step >= 2)(lambda: write(out2))


def project(part, cap, segs, cnts, acts, grads_t, w_in, w_out):
    toks, fa = acts.shape[1:]
    fg = grads_t.shape[1]

    def seg(k):
        return lambda i, s, c: (s[part * 12 + i * SLOTS + k], 0, 0)

    whole = lambda i, s, c: (0, 0)
    out = jax.ShapeDtypeStruct((2 * cap, 128), F32)
    return pl.pallas_call(
        functools.partial(project_kernel, part, cap),
        grid_spec=pltpu.PrefetchScalarGridSpec(
            num_scalar_prefetch=2,
            grid=(4,),
            in_specs=[pl.BlockSpec((1, toks, fa), seg(k)) for k in range(SLOTS)]
            + [pl.BlockSpec((1, fg, toks), seg(k)) for k in range(SLOTS)]
            + [pl.BlockSpec(w_in.shape, whole), pl.BlockSpec(w_out.shape, whole)],
            out_specs=[
                pl.BlockSpec((cap, 128), lambda i, s, c: (jnp.minimum(i, 1), 0)),
                pl.BlockSpec((cap, 128), lambda i, s, c: (jnp.maximum(i - 2, 0), 0)),
            ],
            scratch_shapes=[pltpu.VMEM((toks, 128), F32)],
        ),
        out_shape=(out, out),
        compiler_params=pltpu.CompilerParams(vmem_limit_bytes=24 * 2**20),
        cost_estimate=pl.CostEstimate(
            flops=12 * toks * 2 * 64 * (fa + fg),
            bytes_accessed=12 * toks * 2 * (fa + fg) + 4 * cap * 512,
            transcendentals=0,
        ),
        name="project",
    )(segs, cnts, acts, acts, acts, grads_t, grads_t, grads_t, w_in, w_out)


def split(x):
    hi = x.astype(BF16)
    return hi, (x - hi.astype(F32)).astype(BF16)


def outer_kernel(cnts, own, r1, r2, r3, out, pair):
    total = (own[...] + r1[...]) + (r2[...] + r3[...])
    cap = total.shape[0]
    row = lax.broadcasted_iota(jnp.int32, (cap, 128), 0)
    off1 = up(cnts[0], 8)
    off2 = off1 + up(cnts[1], 8)
    live = [
        row < cnts[0],
        (row >= off1) & (row < off1 + cnts[1]),
        (row >= off2) & (row < off2 + cnts[2]),
    ]
    total = jnp.where(live[0] | live[1] | live[2], total, 0.0)
    lane = lax.broadcasted_iota(jnp.int32, (cap, 128), 1)
    act = jnp.where(lane < 64, pltpu.roll(total, 64, 1), total)
    a_hi, a_lo = split(act)
    total_t = total.T[:64]
    col = lax.broadcasted_iota(jnp.int32, (64, cap), 1)
    live_t = [
        col < cnts[0],
        (col >= off1) & (col < off1 + cnts[1]),
        (col >= off2) & (col < off2 + cnts[2]),
    ]
    grad = jnp.concatenate([jnp.where(m, total_t, 0.0) for m in live_t], axis=0)
    g_hi, g_lo = split(grad)
    dot = functools.partial(jnp.dot, preferred_element_type=F32)
    pair[...] = dot(g_hi, a_hi) + (dot(g_hi, a_lo) + dot(g_lo, a_hi))
    first = pair[pl.ds(0, 96, stride=2), :]
    other = pair[pl.ds(1, 96, stride=2), :]
    lane = lax.broadcasted_iota(jnp.int32, (96, 128), 1)
    out[...] = jnp.where(lane < 64, first, other)


def outer(cnts, parts):
    cap = parts[0].shape[0]
    spec = pl.BlockSpec(memory_space=pltpu.VMEM)
    return pl.pallas_call(
        outer_kernel,
        in_specs=[pl.BlockSpec(memory_space=pltpu.SMEM)] + [spec] * 4,
        out_specs=spec,
        out_shape=jax.ShapeDtypeStruct((SLOTS * 32, 128), F32),
        scratch_shapes=[pltpu.VMEM((SLOTS * 64, 128), F32)],
        compiler_params=pltpu.CompilerParams(vmem_limit_bytes=24 * 2**20),
        cost_estimate=pl.CostEstimate(flops=6 * 192 * cap * 128, bytes_accessed=4 * cap * 512, transcendentals=0),
        name="outer",
    )(cnts, *parts)


def hop(x, pairs):
    return lax.ppermute(x, "rank", pairs)


def features(cap, segs, cnts, acts, grads_t, w_in, w_out):
    made = {}
    got = {}
    for d in (1, 3, 2, 0):
        made[1, d], made[2, d] = project(d, cap, segs, cnts, acts, grads_t, w_in, w_out)
        for role in (1, 2):
            got[role, d] = hop(made[role, d], FIRST[role, d]) if d else made[role, d]
    s1 = (got[1, 0] + got[1, 1]) + (got[1, 3] + got[1, 2])
    s2 = (got[2, 0] + got[2, 1]) + (got[2, 3] + got[2, 2])
    parts = [
        s1[:cap],
        hop(s2[:cap], SECOND[1]),
        hop(s2[cap:], SECOND[2]),
        hop(s1[cap:], SECOND[3]),
    ]
    return outer(cnts[:SLOTS], parts)


def score_kernel(segs, *refs):
    feats, (queries, seg_kind, query_kind, compat, raw_out, sums_out, placed) = refs[:4], refs[4:]
    step = pl.program_id(0)
    n = placed.shape[0]
    nt = (((1,), (1,)), ((), ()))

    @pl.when(step == 0)
    def _():
        placed[...] = jnp.zeros_like(placed)

    dot = functools.partial(lax.dot_general, dimension_numbers=nt, preferred_element_type=F32)
    total = placed[...]
    width = queries.shape[1] // 128
    for m in range(width):
        left = jnp.concatenate(
            [f[pl.ds(step * width + m, f.shape[0] // 32, stride=32), :] for f in feats], axis=0
        )
        l_hi, l_lo = split(left)
        q_hi, q_lo = split(queries[:, m * 128 : (m + 1) * 128])
        both = dot(jnp.concatenate([l_hi, l_lo], axis=0), q_hi)
        total = total + (both[:n] + both[n:]) + dot(l_hi, q_lo)
    placed[...] = total

    @pl.when(step == pl.num_programs(0) - 1)
    def _():
        for slot in range(n):
            raw_out[pl.ds(segs[slot], 1), :] = placed[slot : slot + 1, :]
        kinds = compat.shape[0]
        one_seg = (seg_kind[...] == lax.broadcasted_iota(jnp.int32, (n, kinds), 1)).astype(F32)
        nq = query_kind.shape[1]
        one_query = (query_kind[...] == lax.broadcasted_iota(jnp.int32, (kinds, nq), 0)).astype(F32)
        table = jnp.dot(one_seg, compat[...].astype(F32), preferred_element_type=F32)
        allowed = jnp.dot(table, one_query, preferred_element_type=F32)
        raw = raw_out[...] * allowed
        raw_out[...] = raw
        sums_out[...] = jnp.broadcast_to(jnp.sum(raw * raw, axis=0, keepdims=True), sums_out.shape)


def score(segs, feats, queries, seg_emb, query_emb, compat):
    n, nq = segs.shape[0], queries.shape[0]
    steps = 4
    fixed = lambda i, s: (0, 0)
    return pl.pallas_call(
        score_kernel,
        grid_spec=pltpu.PrefetchScalarGridSpec(
            num_scalar_prefetch=1,
            grid=(steps,),
            in_specs=[pl.BlockSpec(f.shape, fixed) for f in feats]
            + [
                pl.BlockSpec((nq, queries.shape[1] // steps), lambda i, s: (0, i)),
                pl.BlockSpec((n, 1), fixed),
                pl.BlockSpec((1, nq), fixed),
                pl.BlockSpec(compat.shape, fixed),
            ],
            out_specs=[pl.BlockSpec((n, nq), fixed), pl.BlockSpec((8, nq), fixed)],
            scratch_shapes=[pltpu.VMEM((n, nq), F32)],
        ),
        out_shape=(jax.ShapeDtypeStruct((n, nq), F32), jax.ShapeDtypeStruct((8, nq), F32)),
        compiler_params=pltpu.CompilerParams(vmem_limit_bytes=24 * 2**20),
        cost_estimate=pl.CostEstimate(flops=6 * n * nq * 4096, bytes_accessed=nq * 4096 * 4, transcendentals=0),
        name="score",
    )(segs, *feats, queries, seg_emb[:, None], query_emb[None, :], compat)


def per_device(acts, grads, proj_in, proj_out, queries, seg_emb, query_emb, compat, counts):
    segs_here = acts.shape[0]
    me = lax.axis_index("rank")
    grads_t = jnp.swapaxes(grads, 1, 2)
    w_in, w_out = proj_in.T, proj_out.T

    ids = lax.iota(jnp.int32, segs_here)
    before = (counts[None, :] > counts[:, None]) | (
        (counts[None, :] == counts[:, None]) & (ids[None, :] < ids[:, None])
    )
    place = jnp.sum(before.astype(jnp.int32), axis=1)

    def pick(positions, values):
        return jnp.sum(jnp.where(positions[:, None] == place[None, :], values[None, :], 0), axis=1)

    mine = jnp.asarray(PROJECT_POS)[me]
    segs, cnts = pick(mine, ids), pick(mine, counts)
    segs_gathered = pick(jnp.asarray(GATHER_POS)[me], ids)

    owned = features(LADDER[-1], segs, cnts, acts, grads_t, w_in, w_out)
    line = jnp.concatenate([owned] + [hop(owned, shift(d, 0)) for d in (1, 2, 3)], axis=0)
    feats = [line] + [hop(line, shift(0, d)) for d in (1, 2, 3)]
    raw, sums = score(segs_gathered, feats, queries, seg_emb, query_emb, compat)

    cores = 2
    groups = lax.axis_size("dp")
    total = sums + lax.ppermute(sums, "dp", [(i, i ^ 1) for i in range(groups)])
    around = [
        lax.ppermute(total, "dp", [(i, (i + cores * d) % groups) for i in range(groups)])
        for d in range(1, groups // cores)
    ]
    for other in around:
        total = total + other
    power = total[:1] / (segs_here * groups)
    return raw / jnp.sqrt(power + 1e-06)


def solution(mesh):
    return jax.shard_map(
        per_device,
        mesh=mesh,
        in_specs=(
            P("dp", None, "rank"),
            P("dp", None, "rank"),
            P("rank", None),
            P("rank", None),
            P("rank", None),
            P("dp"),
            P("rank"),
            P(),
            P("dp"),
        ),
        out_specs=P("dp", "rank"),
        check_vma=False,
    )
```

```python
import functools

import jax
import jax.numpy as jnp
import numpy as np
from jax import lax
from jax.experimental import pallas as pl
from jax.experimental.pallas import tpu as pltpu
from jax.sharding import PartitionSpec as P

SIDE = 4
RANKS = SIDE * SIDE
SLOTS = 3
BF16 = jnp.bfloat16
F32 = jnp.float32
LADDER = (544, 768)


def at(x, y):
    return (x % SIDE) * SIDE + y % SIDE


def home_x(rank):
    return sum(divmod(rank, SIDE)) % 2 == 0


def neighbour(home, flip, rank):
    x, y = divmod(rank, SIDE)
    return at(x ^ flip, y) if home == home_x(rank) else at(x, y ^ flip)


def stream_owner(home, stream, flip, rank):
    x, y = divmod(rank, SIDE)
    along_x = home == home_x(rank)
    via = neighbour(home, flip, rank)
    if along_x == home_x(via):
        return via if stream == 1 else second(3, via)
    return second(stream, via)


def second(kind, rank):
    x, y = divmod(rank, SIDE)
    even = (x + y) % 2 == 0
    if kind == 3:
        return at(x, y + 2) if even else at(x + 2, y)
    step = 1 if kind == 1 else -1
    return at(x + step, y) if even else at(x, y + step)


def destinations(rank):
    order = []
    for home, stream, flip in BLOCKS:
        order.append(stream_owner(home, stream, flip, rank))
    return order


BLOCKS = (
    [(True, 1, 1), (True, 1, 2), (False, 1, 1), (False, 1, 2)]
    + [(True, 2, 3), (True, 2, 2), (False, 2, 3), (False, 2, 2)]
    + [(True, 1, 3), (True, 2, 1), (False, 1, 3), (False, 2, 1)]
    + [(True, 1, 0), (True, 2, 0), (False, 1, 0), (False, 2, 0)]
)


def slot_positions(rank):
    zig = 7 - rank // 2 if rank % 2 == 0 else 15 - rank // 2
    sums = [r + (7 - r // 2 if r % 2 == 0 else 15 - r // 2) for r in range(RANKS)]
    above = sum(s > sums[rank] or (s == sums[rank] and r > rank) for r, s in enumerate(sums))
    return [rank, RANKS + zig, 2 * RANKS + above]


def gathered(rank):
    x, y = divmod(rank, SIDE)
    return [at(x - dx, y - dy) for dy in range(SIDE) for dx in range(SIDE)]


PROJECT_POS = np.array([sum((slot_positions(q) for q in destinations(r)), []) for r in range(RANKS)], np.int32)
GATHER_POS = np.array([sum((slot_positions(q) for q in gathered(r)), []) for r in range(RANKS)], np.int32)
OWNER_POS = np.array([slot_positions(q) for q in range(RANKS)], np.int32).T.reshape(-1)
FLIPS = {
    (home, flip): [(r, neighbour(home, flip, r)) for r in range(RANKS)] for home in (True, False) for flip in (1, 3)
}
SECOND = {kind: [(r, second(kind, r)) for r in range(RANKS)] for kind in (1, 2, 3)}


def shift(dx, dy):
    return [(r, at(r // SIDE + dx, r % SIDE + dy)) for r in range(RANKS)]


def up(n, m):
    return (n + (m - 1)) // m * m


def project_kernel(first, segs, cnts, acts, grads, w_in, w_out, *refs):
    outs, (act_buf, grad_buf, spill, sems) = refs[:4], refs[4:]
    toks = act_buf.shape[1]
    cap = outs[0].shape[0] // 2

    def copies(j):
        s = segs[first + j]
        return (
            pltpu.make_async_copy(acts.at[s], act_buf.at[j], sems.at[j, 0]),
            pltpu.make_async_copy(grads.at[s], grad_buf.at[j], sems.at[j, 1]),
        )

    for j in range(act_buf.shape[0]):
        for copy in copies(j):
            copy.start()
    w_a = jnp.concatenate([jnp.zeros_like(w_in[...]), w_in[...]], axis=0)
    nt = (((1,), (1,)), ((), ()))

    def rows(j):
        side_g = jnp.dot(w_out[...], grad_buf[j], preferred_element_type=F32)
        side_a = lax.dot_general(act_buf[j], w_a, nt, preferred_element_type=F32)
        return side_a + jnp.concatenate([side_g, jnp.zeros_like(side_g)], axis=0).T

    for h, out in enumerate(outs):

        def block(i, _):
            j = (h * 2 + i) * SLOTS
            for k in range(SLOTS):
                for copy in copies(j + k):
                    copy.wait()
            made = [rows(j + k) for k in range(SLOTS)]
            base = pl.multiple_of(i * cap, 8)
            mid = pl.multiple_of(base + up(cnts[first + j], 8), 8)
            last = pl.multiple_of(mid + up(cnts[first + j + 1], 8), 8)
            out[pl.ds(base, toks), :] = made[0]
            out[pl.ds(mid, toks), :] = made[1]
            spill[...] = made[2]

            def piece(n, _):
                to = pl.multiple_of(last + n * 16, 8)
                out[pl.ds(to, 16), :] = spill[pl.ds(pl.multiple_of(n * 16, 16), 16), :]
                return 0

            return lax.fori_loop(0, up(cnts[first + j + 2], 16) // 16, piece, 0)

        lax.fori_loop(0, 2, block, 0)


def project(part, cap, segs, cnts, acts, grads_t, w_in, w_out):
    toks, fa = acts.shape[1:]
    fg = grads_t.shape[1]
    n = acts.shape[0] // 2
    vmem = pl.BlockSpec(memory_space=pltpu.VMEM)
    smem = pl.BlockSpec(memory_space=pltpu.SMEM)
    any_ = pl.BlockSpec(memory_space=pl.ANY)
    return pl.pallas_call(
        functools.partial(project_kernel, part * n),
        in_specs=[smem, smem, any_, any_, vmem, vmem],
        out_specs=[vmem] * 4,
        out_shape=[jax.ShapeDtypeStruct((2 * cap, 128), F32)] * 4,
        scratch_shapes=[
            pltpu.VMEM((n, toks, fa), BF16),
            pltpu.VMEM((n, fg, toks), BF16),
            pltpu.VMEM((toks, 128), F32),
            pltpu.SemaphoreType.DMA((n, 2)),
        ],
        compiler_params=pltpu.CompilerParams(vmem_limit_bytes=56 * 2**20),
        cost_estimate=pl.CostEstimate(
            flops=n * toks * 2 * 64 * (fa + fg),
            bytes_accessed=n * toks * 2 * (fa + fg) + 8 * cap * 512,
            transcendentals=0,
        ),
        name="project",
    )(segs, cnts, acts, grads_t, w_in, w_out)


def split(x):
    hi = x.astype(BF16)
    return hi, (x - hi.astype(F32)).astype(BF16)


def outer_kernel(cnts, own, r1, r2, r3, out, pair):
    total = (own[...] + r1[...]) + (r2[...] + r3[...])
    cap = total.shape[0]
    row = lax.broadcasted_iota(jnp.int32, (cap, 128), 0)
    off1 = up(cnts[0], 8)
    off2 = off1 + up(cnts[1], 8)
    live = [
        row < cnts[0],
        (row >= off1) & (row < off1 + cnts[1]),
        (row >= off2) & (row < off2 + cnts[2]),
    ]
    total = jnp.where(live[0] | live[1] | live[2], total, 0.0)
    lane = lax.broadcasted_iota(jnp.int32, (cap, 128), 1)
    act = jnp.where(lane < 64, pltpu.roll(total, 64, 1), total)
    a_hi, a_lo = split(act)
    total_t = total.T[:64]
    col = lax.broadcasted_iota(jnp.int32, (64, cap), 1)
    live_t = [
        col < cnts[0],
        (col >= off1) & (col < off1 + cnts[1]),
        (col >= off2) & (col < off2 + cnts[2]),
    ]
    grad = jnp.concatenate([jnp.where(m, total_t, 0.0) for m in live_t], axis=0)
    g_hi, g_lo = split(grad)
    dot = functools.partial(jnp.dot, preferred_element_type=F32)
    pair[...] = dot(g_hi, a_hi) + (dot(g_hi, a_lo) + dot(g_lo, a_hi))
    first = pair[pl.ds(0, 96, stride=2), :]
    other = pair[pl.ds(1, 96, stride=2), :]
    lane = lax.broadcasted_iota(jnp.int32, (96, 128), 1)
    out[...] = jnp.where(lane < 64, first, other)


def outer(cnts, parts):
    cap = parts[0].shape[0]
    spec = pl.BlockSpec(memory_space=pltpu.VMEM)
    return pl.pallas_call(
        outer_kernel,
        in_specs=[pl.BlockSpec(memory_space=pltpu.SMEM)] + [spec] * 4,
        out_specs=spec,
        out_shape=jax.ShapeDtypeStruct((SLOTS * 32, 128), F32),
        scratch_shapes=[pltpu.VMEM((SLOTS * 64, 128), F32)],
        compiler_params=pltpu.CompilerParams(vmem_limit_bytes=24 * 2**20),
        cost_estimate=pl.CostEstimate(flops=6 * 192 * cap * 128, bytes_accessed=4 * cap * 512, transcendentals=0),
        name="outer",
    )(cnts, *parts)


def hop(x, pairs):
    return lax.ppermute(x, "rank", pairs)


def features(cap, segs, cnts, acts, grads_t, w_in, w_out):
    made = [project(part, cap, segs, cnts, acts, grads_t, w_in, w_out) for part in range(2)]
    made = [made[0][:2], made[0][2:], made[1][:2], made[1][2:]]
    flip = {1: 1, 2: 3}
    keep, onward = {}, {}
    for stream in (1, 2):
        for home in (True, False):
            got = hop(made[stream - 1][0 if home else 1], FLIPS[home, flip[stream]])
            at_b = made[2][1 if home else 0][(stream - 1) * cap : stream * cap]
            stay = made[3][1 if home else 0][(stream - 1) * cap : stream * cap]
            onward[not home, stream] = at_b + got[cap:]
            keep[not home, stream] = stay + got[:cap]
    done = {}
    for stream in (1, 2):
        for home in (True, False):
            done[not home, stream] = keep[not home, stream] + hop(onward[home, stream], FLIPS[home, flip[3 - stream]])
    parts = [
        done[True, 1],
        hop(done[False, 1], SECOND[1]),
        hop(done[False, 2], SECOND[2]),
        hop(done[True, 2], SECOND[3]),
    ]
    return outer(cnts[-4 * SLOTS :][:SLOTS], parts)


def score_kernel(segs, *refs):
    feats, (queries, seg_kind, query_kind, compat, raw_out, sums_out, placed) = refs[:4], refs[4:]
    step = pl.program_id(0)
    n = placed.shape[0]
    nt = (((1,), (1,)), ((), ()))

    @pl.when(step == 0)
    def _():
        placed[...] = jnp.zeros_like(placed)

    dot = functools.partial(lax.dot_general, dimension_numbers=nt, preferred_element_type=F32)
    total = placed[...]
    width = queries.shape[1] // 128
    for m in range(width):
        left = jnp.concatenate(
            [f[pl.ds(step * width + m, f.shape[0] // 32, stride=32), :] for f in feats], axis=0
        )
        l_hi, l_lo = split(left)
        q_hi, q_lo = split(queries[:, m * 128 : (m + 1) * 128])
        both = dot(jnp.concatenate([l_hi, l_lo], axis=0), q_hi)
        total = total + (both[:n] + both[n:]) + dot(l_hi, q_lo)
    placed[...] = total

    @pl.when(step == pl.num_programs(0) - 1)
    def _():
        for slot in range(n):
            raw_out[pl.ds(segs[slot], 1), :] = placed[slot : slot + 1, :]
        kinds = compat.shape[0]
        one_seg = (seg_kind[...] == lax.broadcasted_iota(jnp.int32, (n, kinds), 1)).astype(F32)
        nq = query_kind.shape[1]
        one_query = (query_kind[...] == lax.broadcasted_iota(jnp.int32, (kinds, nq), 0)).astype(F32)
        table = jnp.dot(one_seg, compat[...].astype(F32), preferred_element_type=F32)
        allowed = jnp.dot(table, one_query, preferred_element_type=F32)
        raw = raw_out[...] * allowed
        raw_out[...] = raw
        sums_out[...] = jnp.broadcast_to(jnp.sum(raw * raw, axis=0, keepdims=True), sums_out.shape)


def score(segs, feats, queries, seg_emb, query_emb, compat):
    n, nq = segs.shape[0], queries.shape[0]
    steps = 4
    fixed = lambda i, s: (0, 0)
    return pl.pallas_call(
        score_kernel,
        grid_spec=pltpu.PrefetchScalarGridSpec(
            num_scalar_prefetch=1,
            grid=(steps,),
            in_specs=[pl.BlockSpec(f.shape, fixed) for f in feats]
            + [
                pl.BlockSpec((nq, queries.shape[1] // steps), lambda i, s: (0, i)),
                pl.BlockSpec((n, 1), fixed),
                pl.BlockSpec((1, nq), fixed),
                pl.BlockSpec(compat.shape, fixed),
            ],
            out_specs=[pl.BlockSpec((n, nq), fixed), pl.BlockSpec((8, nq), fixed)],
            scratch_shapes=[pltpu.VMEM((n, nq), F32)],
        ),
        out_shape=(jax.ShapeDtypeStruct((n, nq), F32), jax.ShapeDtypeStruct((8, nq), F32)),
        compiler_params=pltpu.CompilerParams(vmem_limit_bytes=24 * 2**20),
        cost_estimate=pl.CostEstimate(flops=6 * n * nq * 4096, bytes_accessed=nq * 4096 * 4, transcendentals=0),
        name="score",
    )(segs, *feats, queries, seg_emb[:, None], query_emb[None, :], compat)


def per_device(acts, grads, proj_in, proj_out, queries, seg_emb, query_emb, compat, counts):
    segs_here = acts.shape[0]
    me = lax.axis_index("rank")
    grads_t = jnp.swapaxes(grads, 1, 2)
    w_in, w_out = proj_in.T, proj_out.T

    ids = lax.iota(jnp.int32, segs_here)
    before = (counts[None, :] > counts[:, None]) | (
        (counts[None, :] == counts[:, None]) & (ids[None, :] < ids[:, None])
    )
    place = jnp.sum(before.astype(jnp.int32), axis=1)

    def pick(positions, values):
        return jnp.sum(jnp.where(positions[:, None] == place[None, :], values[None, :], 0), axis=1)

    mine = jnp.asarray(PROJECT_POS)[me]
    segs, cnts = pick(mine, ids), pick(mine, counts)
    segs_gathered = pick(jnp.asarray(GATHER_POS)[me], ids)

    held = pick(jnp.asarray(OWNER_POS), counts).reshape(SLOTS, RANKS)
    need = jnp.max(up(held[0], 8) + up(held[1], 8) + up(held[2], 16))
    rung = jnp.sum((need > jnp.asarray(LADDER[:-1])).astype(jnp.int32))
    branches = [functools.partial(features, cap) for cap in LADDER]
    owned = lax.switch(rung, branches, segs, cnts, acts, grads_t, w_in, w_out)
    line = jnp.concatenate([owned] + [hop(owned, shift(d, 0)) for d in (1, 2, 3)], axis=0)
    feats = [line] + [hop(line, shift(0, d)) for d in (1, 2, 3)]
    groups = lax.axis_size("dp")
    raw, sums = score(segs_gathered, feats, queries, seg_emb, query_emb, compat)

    total = sums
    for core, z in ((1, 0), (0, 1), (0, 3)):
        other = [(i, (i // 2 ^ z) * 2 + (i % 2 ^ core)) for i in range(groups)]
        total = total + lax.ppermute(total, "dp", other)
    power = total[:1] / (segs_here * groups)
    return raw / jnp.sqrt(power + 1e-06)


def solution(mesh):
    return jax.shard_map(
        per_device,
        mesh=mesh,
        in_specs=(
            P("dp", None, "rank"),
            P("dp", None, "rank"),
            P("rank", None),
            P("rank", None),
            P("rank", None),
            P("dp"),
            P("rank"),
            P(),
            P("dp"),
        ),
        out_specs=P("dp", "rank"),
        check_vma=False,
    )
```

```python
import functools

import jax
import jax.numpy as jnp
import numpy as np
from jax import lax
from jax.experimental import pallas as pl
from jax.experimental.pallas import tpu as pltpu
from jax.sharding import PartitionSpec as P

SIDE = 4
RANKS = SIDE * SIDE
SLOTS = 3
BF16 = jnp.bfloat16
F32 = jnp.float32
LADDER = (544, 768)


def at(x, y):
    return (x % SIDE) * SIDE + y % SIDE


def home_x(rank):
    return sum(divmod(rank, SIDE)) % 2 == 0


def neighbour(home, flip, rank):
    x, y = divmod(rank, SIDE)
    return at(x ^ flip, y) if home == home_x(rank) else at(x, y ^ flip)


def stream_owner(home, stream, flip, rank):
    x, y = divmod(rank, SIDE)
    along_x = home == home_x(rank)
    via = neighbour(home, flip, rank)
    if along_x == home_x(via):
        return via if stream == 1 else second(3, via)
    return second(stream, via)


def second(kind, rank):
    x, y = divmod(rank, SIDE)
    even = (x + y) % 2 == 0
    if kind == 3:
        return at(x, y + 2) if even else at(x + 2, y)
    step = 1 if kind == 1 else -1
    return at(x + step, y) if even else at(x, y + step)


def destinations(rank):
    order = []
    for home, stream, flip in BLOCKS:
        order.append(stream_owner(home, stream, flip, rank))
    return order


BLOCKS = (
    [(True, 1, 1), (True, 1, 2), (False, 1, 1), (False, 1, 2)]
    + [(True, 2, 3), (True, 2, 2), (False, 2, 3), (False, 2, 2)]
    + [(True, 1, 3), (True, 2, 1), (False, 1, 3), (False, 2, 1)]
    + [(True, 1, 0), (True, 2, 0), (False, 1, 0), (False, 2, 0)]
)


def slot_positions(rank):
    zig = 7 - rank // 2 if rank % 2 == 0 else 15 - rank // 2
    sums = [r + (7 - r // 2 if r % 2 == 0 else 15 - r // 2) for r in range(RANKS)]
    above = sum(s > sums[rank] or (s == sums[rank] and r > rank) for r, s in enumerate(sums))
    return [rank, RANKS + zig, 2 * RANKS + above]


def gathered(rank):
    x, y = divmod(rank, SIDE)
    return [at(x - dx, y - dy) for dy in range(SIDE) for dx in range(SIDE)]


PROJECT_POS = np.array([sum((slot_positions(q) for q in destinations(r)), []) for r in range(RANKS)], np.int32)
GATHER_POS = np.array([sum((slot_positions(q) for q in gathered(r)), []) for r in range(RANKS)], np.int32)
OWNER_POS = np.array([slot_positions(q) for q in range(RANKS)], np.int32).T.reshape(-1)
FLIPS = {
    (home, flip): [(r, neighbour(home, flip, r)) for r in range(RANKS)] for home in (True, False) for flip in (1, 3)
}
SECOND = {kind: [(r, second(kind, r)) for r in range(RANKS)] for kind in (1, 2, 3)}


def shift(dx, dy):
    return [(r, at(r // SIDE + dx, r % SIDE + dy)) for r in range(RANKS)]


def up(n, m):
    return (n + (m - 1)) // m * m


def project_kernel(first, segs, cnts, acts, grads, w_in, w_out, *refs):
    outs, (act_buf, grad_buf, spill, sems) = refs[:4], refs[4:]
    toks = act_buf.shape[1]
    cap = outs[0].shape[0] // 2

    def copies(j):
        s = segs[first + j]
        return (
            pltpu.make_async_copy(acts.at[s], act_buf.at[j], sems.at[j, 0]),
            pltpu.make_async_copy(grads.at[s], grad_buf.at[j], sems.at[j, 1]),
        )

    for j in range(act_buf.shape[0]):
        for copy in copies(j):
            copy.start()
    w_a = jnp.concatenate([jnp.zeros_like(w_in[...]), w_in[...]], axis=0)
    nt = (((1,), (1,)), ((), ()))

    def rows(j):
        side_g = jnp.dot(w_out[...], grad_buf[j], preferred_element_type=F32)
        side_a = lax.dot_general(act_buf[j], w_a, nt, preferred_element_type=F32)
        return side_a + jnp.concatenate([side_g, jnp.zeros_like(side_g)], axis=0).T

    for h, out in enumerate(outs):

        def block(i, _):
            j = (h * 2 + i) * SLOTS
            for k in range(SLOTS):
                for copy in copies(j + k):
                    copy.wait()
            made = [rows(j + k) for k in range(SLOTS)]
            base = pl.multiple_of(i * cap, 8)
            mid = pl.multiple_of(base + up(cnts[first + j], 8), 8)
            last = pl.multiple_of(mid + up(cnts[first + j + 1], 8), 8)
            out[pl.ds(base, toks), :] = made[0]
            out[pl.ds(mid, toks), :] = made[1]
            spill[...] = made[2]

            def piece(n, _):
                to = pl.multiple_of(last + n * 16, 8)
                out[pl.ds(to, 16), :] = spill[pl.ds(pl.multiple_of(n * 16, 16), 16), :]
                return 0

            return lax.fori_loop(0, up(cnts[first + j + 2], 16) // 16, piece, 0)

        lax.fori_loop(0, 2, block, 0)


def project(part, cap, segs, cnts, acts, grads_t, w_in, w_out):
    toks, fa = acts.shape[1:]
    fg = grads_t.shape[1]
    n = acts.shape[0] // 2
    vmem = pl.BlockSpec(memory_space=pltpu.VMEM)
    smem = pl.BlockSpec(memory_space=pltpu.SMEM)
    any_ = pl.BlockSpec(memory_space=pl.ANY)
    return pl.pallas_call(
        functools.partial(project_kernel, part * n),
        in_specs=[smem, smem, any_, any_, vmem, vmem],
        out_specs=[vmem] * 4,
        out_shape=[jax.ShapeDtypeStruct((2 * cap, 128), F32)] * 4,
        scratch_shapes=[
            pltpu.VMEM((n, toks, fa), BF16),
            pltpu.VMEM((n, fg, toks), BF16),
            pltpu.VMEM((toks, 128), F32),
            pltpu.SemaphoreType.DMA((n, 2)),
        ],
        compiler_params=pltpu.CompilerParams(vmem_limit_bytes=56 * 2**20),
        cost_estimate=pl.CostEstimate(
            flops=n * toks * 2 * 64 * (fa + fg),
            bytes_accessed=n * toks * 2 * (fa + fg) + 8 * cap * 512,
            transcendentals=0,
        ),
        name="project",
    )(segs, cnts, acts, grads_t, w_in, w_out)


def split(x):
    hi = x.astype(BF16)
    return hi, (x - hi.astype(F32)).astype(BF16)


def outer_kernel(cnts, own, r1, r2, r3, out, pair):
    total = (own[...] + r1[...]) + (r2[...] + r3[...])
    cap = total.shape[0]
    row = lax.broadcasted_iota(jnp.int32, (cap, 128), 0)
    off1 = up(cnts[0], 8)
    off2 = off1 + up(cnts[1], 8)
    live = [
        row < cnts[0],
        (row >= off1) & (row < off1 + cnts[1]),
        (row >= off2) & (row < off2 + cnts[2]),
    ]
    total = jnp.where(live[0] | live[1] | live[2], total, 0.0)
    lane = lax.broadcasted_iota(jnp.int32, (cap, 128), 1)
    act = jnp.where(lane < 64, pltpu.roll(total, 64, 1), total)
    a_hi, a_lo = split(act)
    total_t = total.T[:64]
    col = lax.broadcasted_iota(jnp.int32, (64, cap), 1)
    live_t = [
        col < cnts[0],
        (col >= off1) & (col < off1 + cnts[1]),
        (col >= off2) & (col < off2 + cnts[2]),
    ]
    grad = jnp.concatenate([jnp.where(m, total_t, 0.0) for m in live_t], axis=0)
    g_hi, g_lo = split(grad)
    dot = functools.partial(jnp.dot, preferred_element_type=F32)
    pair[...] = dot(g_hi, a_hi) + (dot(g_hi, a_lo) + dot(g_lo, a_hi))
    first = pair[pl.ds(0, 96, stride=2), :]
    other = pair[pl.ds(1, 96, stride=2), :]
    lane = lax.broadcasted_iota(jnp.int32, (96, 128), 1)
    out[...] = jnp.where(lane < 64, first, other)


def outer(cnts, parts):
    cap = parts[0].shape[0]
    spec = pl.BlockSpec(memory_space=pltpu.VMEM)
    return pl.pallas_call(
        outer_kernel,
        in_specs=[pl.BlockSpec(memory_space=pltpu.SMEM)] + [spec] * 4,
        out_specs=spec,
        out_shape=jax.ShapeDtypeStruct((SLOTS * 32, 128), F32),
        scratch_shapes=[pltpu.VMEM((SLOTS * 64, 128), F32)],
        compiler_params=pltpu.CompilerParams(vmem_limit_bytes=24 * 2**20),
        cost_estimate=pl.CostEstimate(flops=6 * 192 * cap * 128, bytes_accessed=4 * cap * 512, transcendentals=0),
        name="outer",
    )(cnts, *parts)


def hop(x, pairs):
    return lax.ppermute(x, "rank", pairs)


def features(cap, segs, cnts, acts, grads_t, w_in, w_out):
    made = [project(part, cap, segs, cnts, acts, grads_t, w_in, w_out) for part in range(2)]
    made = [made[0][:2], made[0][2:], made[1][:2], made[1][2:]]
    flip = {1: 1, 2: 3}
    orders = [(stream, home) for stream in (1, 2) for home in (True, False)]
    got, onward, done = {}, {}, {}
    for stream, home in orders:
        got[not home, stream] = hop(made[stream - 1][0 if home else 1], FLIPS[home, flip[stream]])
    came = {}
    for stream, home in orders:
        at_b = made[2][0 if home else 1][(stream - 1) * cap : stream * cap]
        onward[home, stream] = at_b + got[home, stream][cap:]
        came[not home, stream] = hop(onward[home, stream], FLIPS[home, flip[3 - stream]])
    came[True, 1], came[False, 1], _, _ = lax.optimization_barrier(
        (came[True, 1], came[False, 1], onward[True, 2], onward[False, 2])
    )
    for stream, home in orders:
        stay = made[3][0 if home else 1][(stream - 1) * cap : stream * cap]
        done[home, stream] = (stay + got[home, stream][:cap]) + came[home, stream]
    parts = [
        done[True, 1],
        hop(done[False, 1], SECOND[1]),
        hop(done[False, 2], SECOND[2]),
        hop(done[True, 2], SECOND[3]),
    ]
    return outer(cnts[-4 * SLOTS :][:SLOTS], parts)


def halves_kernel(queries, hi, lo):
    hi[...], lo[...] = split(queries[...])


def halves(queries):
    nq, nf = queries.shape
    steps = 4
    spec = pl.BlockSpec((nq // steps, nf), lambda i: (i, 0))
    out = jax.ShapeDtypeStruct((nq, nf), BF16)
    return pl.pallas_call(
        halves_kernel,
        grid=(steps,),
        in_specs=[spec],
        out_specs=[spec, spec],
        out_shape=[out, out],
        compiler_params=pltpu.CompilerParams(vmem_limit_bytes=48 * 2**20),
        cost_estimate=pl.CostEstimate(flops=nq * nf * 2, bytes_accessed=nq * nf * 8, transcendentals=0),
        name="halves",
    )(queries)


def score_kernel(segs, *refs):
    feats, (q_hi, q_lo, seg_kind, query_kind, compat, raw_out, sums_out, placed) = refs[:4], refs[4:]
    n = placed.shape[0]
    nt = (((1,), (1,)), ((), ()))
    dot = functools.partial(lax.dot_general, dimension_numbers=nt, preferred_element_type=F32)
    width = q_hi.shape[1] // 128
    total = jnp.zeros(placed.shape, F32)
    for m in range(0, width, 2):
        left = jnp.concatenate(
            [
                jnp.concatenate([f[pl.ds(m + e, f.shape[0] // width, stride=width), :] for f in feats], axis=0)
                for e in range(2)
            ],
            axis=1,
        )
        l_hi, l_lo = split(left)
        cols = slice(m * 128, (m + 2) * 128)
        both = dot(jnp.concatenate([l_hi, l_lo], axis=0), q_hi[:, cols])
        total = total + ((both[:n] + both[n:]) + dot(l_hi, q_lo[:, cols]))
    placed[...] = total
    for slot in range(n):
        raw_out[pl.ds(segs[slot], 1), :] = placed[slot : slot + 1, :]
    kinds = compat.shape[0]
    one_seg = (seg_kind[...] == lax.broadcasted_iota(jnp.int32, (n, kinds), 1)).astype(F32)
    nq = query_kind.shape[1]
    one_query = (query_kind[...] == lax.broadcasted_iota(jnp.int32, (kinds, nq), 0)).astype(F32)
    table = jnp.dot(one_seg, compat[...].astype(F32), preferred_element_type=F32)
    allowed = jnp.dot(table, one_query, preferred_element_type=F32)
    raw = raw_out[...] * allowed
    raw_out[...] = raw
    sums_out[...] = jnp.broadcast_to(jnp.sum(raw * raw, axis=0, keepdims=True), sums_out.shape)


def score(segs, feats, q_hi, q_lo, seg_emb, query_emb, compat):
    n, (nq, nf) = segs.shape[0], q_hi.shape
    vmem = pl.BlockSpec(memory_space=pltpu.VMEM)
    return pl.pallas_call(
        score_kernel,
        in_specs=[pl.BlockSpec(memory_space=pltpu.SMEM)] + [vmem] * 9,
        out_specs=[vmem, vmem],
        out_shape=(jax.ShapeDtypeStruct((n, nq), F32), jax.ShapeDtypeStruct((8, nq), F32)),
        scratch_shapes=[pltpu.VMEM((n, nq), F32)],
        compiler_params=pltpu.CompilerParams(vmem_limit_bytes=24 * 2**20),
        cost_estimate=pl.CostEstimate(flops=6 * n * nq * nf, bytes_accessed=nq * nf * 4, transcendentals=0),
        name="score",
    )(segs, *feats, q_hi, q_lo, seg_emb[:, None], query_emb[None, :], compat)


def per_device(acts, grads, proj_in, proj_out, queries, seg_emb, query_emb, compat, counts):
    segs_here = acts.shape[0]
    me = lax.axis_index("rank")
    grads_t = jnp.swapaxes(grads, 1, 2)
    w_in, w_out = proj_in.T, proj_out.T

    ids = lax.iota(jnp.int32, segs_here)
    before = (counts[None, :] > counts[:, None]) | (
        (counts[None, :] == counts[:, None]) & (ids[None, :] < ids[:, None])
    )
    place = jnp.sum(before.astype(jnp.int32), axis=1)

    def pick(positions, values):
        return jnp.sum(jnp.where(positions[:, None] == place[None, :], values[None, :], 0), axis=1)

    mine = jnp.asarray(PROJECT_POS)[me]
    segs, cnts = pick(mine, ids), pick(mine, counts)
    segs_gathered = pick(jnp.asarray(GATHER_POS)[me], ids)

    held = pick(jnp.asarray(OWNER_POS), counts).reshape(SLOTS, RANKS)
    need = jnp.max(up(held[0], 8) + up(held[1], 8) + up(held[2], 16))
    rung = jnp.sum((need > jnp.asarray(LADDER[:-1])).astype(jnp.int32))
    branches = [functools.partial(features, cap) for cap in LADDER]
    owned = lax.switch(rung, branches, segs, cnts, acts, grads_t, w_in, w_out)
    queries, owned = lax.optimization_barrier((queries, owned))
    q_hi, q_lo = halves(queries)
    line = jnp.concatenate([owned] + [hop(owned, shift(d, 0)) for d in (1, 2, 3)], axis=0)
    feats = [line] + [hop(line, shift(0, d)) for d in (1, 2, 3)]
    groups = lax.axis_size("dp")
    raw, sums = score(segs_gathered, feats, q_hi, q_lo, seg_emb, query_emb, compat)

    total = sums
    for core, z in ((1, 0), (0, 1), (0, 3)):
        other = [(i, (i // 2 ^ z) * 2 + (i % 2 ^ core)) for i in range(groups)]
        total = total + lax.ppermute(total, "dp", other)
    power = total[:1] / (segs_here * groups)
    return raw / jnp.sqrt(power + 1e-06)


def solution(mesh):
    return jax.shard_map(
        per_device,
        mesh=mesh,
        in_specs=(
            P("dp", None, "rank"),
            P("dp", None, "rank"),
            P("rank", None),
            P("rank", None),
            P("rank", None),
            P("dp"),
            P("rank"),
            P(),
            P("dp"),
        ),
        out_specs=P("dp", "rank"),
        check_vma=False,
    )
```

```python
import functools

import jax
import jax.numpy as jnp
import numpy as np
from jax import lax
from jax.experimental import pallas as pl
from jax.experimental.pallas import tpu as pltpu
from jax.sharding import PartitionSpec as P

SIDE = 4
RANKS = SIDE * SIDE
SLOTS = 3
BF16 = jnp.bfloat16
F32 = jnp.float32
LADDER = (544, 768)


def at(x, y):
    return (x % SIDE) * SIDE + y % SIDE


def home_x(rank):
    return sum(divmod(rank, SIDE)) % 2 == 0


def neighbour(home, flip, rank):
    x, y = divmod(rank, SIDE)
    return at(x ^ flip, y) if home == home_x(rank) else at(x, y ^ flip)


def stream_owner(home, stream, flip, rank):
    x, y = divmod(rank, SIDE)
    along_x = home == home_x(rank)
    via = neighbour(home, flip, rank)
    if along_x == home_x(via):
        return via if stream == 1 else second(3, via)
    return second(stream, via)


def second(kind, rank):
    x, y = divmod(rank, SIDE)
    even = (x + y) % 2 == 0
    if kind == 3:
        return at(x, y + 2) if even else at(x + 2, y)
    step = 1 if kind == 1 else -1
    return at(x + step, y) if even else at(x, y + step)


def destinations(rank):
    order = []
    for home, stream, flip in BLOCKS:
        order.append(stream_owner(home, stream, flip, rank))
    return order


BLOCKS = (
    [(True, 1, 1), (True, 1, 2), (False, 1, 1), (False, 1, 2)]
    + [(True, 2, 3), (True, 2, 2), (False, 2, 3), (False, 2, 2)]
    + [(True, 1, 3), (True, 2, 1), (False, 1, 3), (False, 2, 1)]
    + [(True, 1, 0), (True, 2, 0), (False, 1, 0), (False, 2, 0)]
)


def slot_positions(rank):
    zig = 7 - rank // 2 if rank % 2 == 0 else 15 - rank // 2
    sums = [r + (7 - r // 2 if r % 2 == 0 else 15 - r // 2) for r in range(RANKS)]
    above = sum(s > sums[rank] or (s == sums[rank] and r > rank) for r, s in enumerate(sums))
    return [rank, RANKS + zig, 2 * RANKS + above]


def gathered(rank):
    x, y = divmod(rank, SIDE)
    return [at(x - dx, y - dy) for dy in range(SIDE) for dx in range(SIDE)]


PROJECT_POS = np.array([sum((slot_positions(q) for q in destinations(r)), []) for r in range(RANKS)], np.int32)
GATHER_POS = np.array([sum((slot_positions(q) for q in gathered(r)), []) for r in range(RANKS)], np.int32)
OWNER_POS = np.array([slot_positions(q) for q in range(RANKS)], np.int32).T.reshape(-1)
FLIPS = {
    (home, flip): [(r, neighbour(home, flip, r)) for r in range(RANKS)] for home in (True, False) for flip in (1, 3)
}
SECOND = {kind: [(r, second(kind, r)) for r in range(RANKS)] for kind in (1, 2, 3)}


def shift(dx, dy):
    return [(r, at(r // SIDE + dx, r % SIDE + dy)) for r in range(RANKS)]


def up(n, m):
    return (n + (m - 1)) // m * m


def project_kernel(first, segs, cnts, acts, grads, w_in, w_out, *refs):
    outs, (act_buf, grad_buf, made_buf, spill, sems, out_sems) = refs[:4], refs[4:]
    toks = act_buf.shape[1]
    cap = outs[0].shape[0] // 2

    def copies(j):
        s = segs[first + j]
        return (
            pltpu.make_async_copy(acts.at[s], act_buf.at[j], sems.at[j, 0]),
            pltpu.make_async_copy(grads.at[s], grad_buf.at[j], sems.at[j, 1]),
        )

    for j in range(act_buf.shape[0]):
        for copy in copies(j):
            copy.start()
    w_a = jnp.concatenate([jnp.zeros_like(w_in[...]), w_in[...]], axis=0)
    nt = (((1,), (1,)), ((), ()))

    def rows(j):
        side_g = jnp.dot(w_out[...], grad_buf[j], preferred_element_type=F32)
        side_a = lax.dot_general(act_buf[j], w_a, nt, preferred_element_type=F32)
        return side_a + jnp.concatenate([side_g, jnp.zeros_like(side_g)], axis=0).T

    leaving = []
    for h in range(len(outs)):
        out = made_buf.at[h]

        def block(i, _):
            j = (h * 2 + i) * SLOTS
            for k in range(SLOTS):
                for copy in copies(j + k):
                    copy.wait()
            made = [rows(j + k) for k in range(SLOTS)]
            base = pl.multiple_of(i * cap, 8)
            mid = pl.multiple_of(base + up(cnts[first + j], 8), 8)
            last = pl.multiple_of(mid + up(cnts[first + j + 1], 8), 8)
            out[pl.ds(base, toks), :] = made[0]
            out[pl.ds(mid, toks), :] = made[1]
            spill[...] = made[2]

            def piece(n, _):
                to = pl.multiple_of(last + n * 16, 8)
                out[pl.ds(to, 16), :] = spill[pl.ds(pl.multiple_of(n * 16, 16), 16), :]
                return 0

            return lax.fori_loop(0, up(cnts[first + j + 2], 16) // 16, piece, 0)

        lax.fori_loop(0, 2, block, 0)
        leaving.append(pltpu.make_async_copy(out, outs[h], out_sems.at[h]))
        leaving[-1].start()
    for copy in leaving:
        copy.wait()


def project(part, cap, segs, cnts, acts, grads_t, w_in, w_out):
    toks, fa = acts.shape[1:]
    fg = grads_t.shape[1]
    n = acts.shape[0] // 2
    vmem = pl.BlockSpec(memory_space=pltpu.VMEM)
    smem = pl.BlockSpec(memory_space=pltpu.SMEM)
    any_ = pl.BlockSpec(memory_space=pl.ANY)
    return pl.pallas_call(
        functools.partial(project_kernel, part * n),
        in_specs=[smem, smem, any_, any_, vmem, vmem],
        out_specs=[any_] * 4,
        out_shape=[jax.ShapeDtypeStruct((2 * cap, 128), F32)] * 4,
        scratch_shapes=[
            pltpu.VMEM((n, toks, fa), BF16),
            pltpu.VMEM((n, fg, toks), BF16),
            pltpu.VMEM((4, 2 * cap, 128), F32),
            pltpu.VMEM((toks, 128), F32),
            pltpu.SemaphoreType.DMA((n, 2)),
            pltpu.SemaphoreType.DMA((4,)),
        ],
        compiler_params=pltpu.CompilerParams(vmem_limit_bytes=40 * 2**20),
        cost_estimate=pl.CostEstimate(
            flops=n * toks * 2 * 64 * (fa + fg),
            bytes_accessed=n * toks * 2 * (fa + fg) + 8 * cap * 512,
            transcendentals=0,
        ),
        name="project",
    )(segs, cnts, acts, grads_t, w_in, w_out)


def split(x):
    hi = x.astype(BF16)
    return hi, (x - hi.astype(F32)).astype(BF16)


def outer_kernel(cnts, own, r1, r2, r3, out, pair):
    total = (own[...] + r1[...]) + (r2[...] + r3[...])
    cap = total.shape[0]
    row = lax.broadcasted_iota(jnp.int32, (cap, 128), 0)
    off1 = up(cnts[0], 8)
    off2 = off1 + up(cnts[1], 8)
    live = [
        row < cnts[0],
        (row >= off1) & (row < off1 + cnts[1]),
        (row >= off2) & (row < off2 + cnts[2]),
    ]
    total = jnp.where(live[0] | live[1] | live[2], total, 0.0)
    lane = lax.broadcasted_iota(jnp.int32, (cap, 128), 1)
    act = jnp.where(lane < 64, pltpu.roll(total, 64, 1), total)
    a_hi, a_lo = split(act)
    total_t = total.T[:64]
    col = lax.broadcasted_iota(jnp.int32, (64, cap), 1)
    live_t = [
        col < cnts[0],
        (col >= off1) & (col < off1 + cnts[1]),
        (col >= off2) & (col < off2 + cnts[2]),
    ]
    grad = jnp.concatenate([jnp.where(m, total_t, 0.0) for m in live_t], axis=0)
    g_hi, g_lo = split(grad)
    dot = functools.partial(jnp.dot, preferred_element_type=F32)
    pair[...] = dot(g_hi, a_hi) + (dot(g_hi, a_lo) + dot(g_lo, a_hi))
    first = pair[pl.ds(0, 96, stride=2), :]
    other = pair[pl.ds(1, 96, stride=2), :]
    lane = lax.broadcasted_iota(jnp.int32, (96, 128), 1)
    out[...] = jnp.where(lane < 64, first, other)


def outer(cnts, parts):
    cap = parts[0].shape[0]
    spec = pl.BlockSpec(memory_space=pltpu.VMEM)
    return pl.pallas_call(
        outer_kernel,
        in_specs=[pl.BlockSpec(memory_space=pltpu.SMEM)] + [spec] * 4,
        out_specs=spec,
        out_shape=jax.ShapeDtypeStruct((SLOTS * 32, 128), F32),
        scratch_shapes=[pltpu.VMEM((SLOTS * 64, 128), F32)],
        compiler_params=pltpu.CompilerParams(vmem_limit_bytes=24 * 2**20),
        cost_estimate=pl.CostEstimate(flops=6 * 192 * cap * 128, bytes_accessed=4 * cap * 512, transcendentals=0),
        name="outer",
    )(cnts, *parts)


def hop(x, pairs):
    return lax.ppermute(x, "rank", pairs)


def features(cap, segs, cnts, acts, grads_t, w_in, w_out):
    made = [project(part, cap, segs, cnts, acts, grads_t, w_in, w_out) for part in range(2)]
    made = [made[0][:2], made[0][2:], made[1][:2], made[1][2:]]
    flip = {1: 1, 2: 3}
    orders = [(stream, home) for stream in (1, 2) for home in (True, False)]
    got, onward, done = {}, {}, {}
    for stream, home in orders:
        got[not home, stream] = hop(made[stream - 1][0 if home else 1], FLIPS[home, flip[stream]])
    came = {}
    for stream, home in orders:
        at_b = made[2][0 if home else 1][(stream - 1) * cap : stream * cap]
        onward[home, stream] = at_b + got[home, stream][cap:]
        came[not home, stream] = hop(onward[home, stream], FLIPS[home, flip[3 - stream]])
    came[True, 1], came[False, 1], _, _ = lax.optimization_barrier(
        (came[True, 1], came[False, 1], onward[True, 2], onward[False, 2])
    )
    for stream, home in orders:
        stay = made[3][0 if home else 1][(stream - 1) * cap : stream * cap]
        done[home, stream] = (stay + got[home, stream][:cap]) + came[home, stream]
    parts = [
        done[True, 1],
        hop(done[False, 1], SECOND[1]),
        hop(done[False, 2], SECOND[2]),
        hop(done[True, 2], SECOND[3]),
    ]
    return outer(cnts[-4 * SLOTS :][:SLOTS], parts)


def halves_kernel(queries, hi, lo):
    hi[...], lo[...] = split(queries[...])


def halves(queries):
    nq, nf = queries.shape
    steps = 4
    spec = pl.BlockSpec((nq // steps, nf), lambda i: (i, 0))
    out = jax.ShapeDtypeStruct((nq, nf), BF16)
    return pl.pallas_call(
        halves_kernel,
        grid=(steps,),
        in_specs=[spec],
        out_specs=[spec, spec],
        out_shape=[out, out],
        compiler_params=pltpu.CompilerParams(vmem_limit_bytes=48 * 2**20),
        cost_estimate=pl.CostEstimate(flops=nq * nf * 2, bytes_accessed=nq * nf * 8, transcendentals=0),
        name="halves",
    )(queries)


def score_kernel(segs, *refs):
    feats, (q_hi, q_lo, seg_kind, query_kind, compat, raw_out, sums_out, placed) = refs[:4], refs[4:]
    n = placed.shape[0]
    nt = (((1,), (1,)), ((), ()))
    dot = functools.partial(lax.dot_general, dimension_numbers=nt, preferred_element_type=F32)
    width = q_hi.shape[1] // 128
    total = jnp.zeros(placed.shape, F32)
    for m in range(0, width, 2):
        left = jnp.concatenate(
            [
                jnp.concatenate([f[pl.ds(m + e, f.shape[0] // width, stride=width), :] for f in feats], axis=0)
                for e in range(2)
            ],
            axis=1,
        )
        l_hi, l_lo = split(left)
        cols = slice(m * 128, (m + 2) * 128)
        both = dot(jnp.concatenate([l_hi, l_lo], axis=0), q_hi[:, cols])
        total = total + ((both[:n] + both[n:]) + dot(l_hi, q_lo[:, cols]))
    placed[...] = total
    for slot in range(n):
        raw_out[pl.ds(segs[slot], 1), :] = placed[slot : slot + 1, :]
    kinds = compat.shape[0]
    one_seg = (seg_kind[...] == lax.broadcasted_iota(jnp.int32, (n, kinds), 1)).astype(F32)
    nq = query_kind.shape[1]
    one_query = (query_kind[...] == lax.broadcasted_iota(jnp.int32, (kinds, nq), 0)).astype(F32)
    table = jnp.dot(one_seg, compat[...].astype(F32), preferred_element_type=F32)
    allowed = jnp.dot(table, one_query, preferred_element_type=F32)
    raw = raw_out[...] * allowed
    raw_out[...] = raw
    sums_out[...] = jnp.broadcast_to(jnp.sum(raw * raw, axis=0, keepdims=True), sums_out.shape)


def score(segs, feats, q_hi, q_lo, seg_emb, query_emb, compat):
    n, (nq, nf) = segs.shape[0], q_hi.shape
    vmem = pl.BlockSpec(memory_space=pltpu.VMEM)
    return pl.pallas_call(
        score_kernel,
        in_specs=[pl.BlockSpec(memory_space=pltpu.SMEM)] + [vmem] * 9,
        out_specs=[vmem, vmem],
        out_shape=(jax.ShapeDtypeStruct((n, nq), F32), jax.ShapeDtypeStruct((8, nq), F32)),
        scratch_shapes=[pltpu.VMEM((n, nq), F32)],
        compiler_params=pltpu.CompilerParams(vmem_limit_bytes=24 * 2**20),
        cost_estimate=pl.CostEstimate(flops=6 * n * nq * nf, bytes_accessed=nq * nf * 4, transcendentals=0),
        name="score",
    )(segs, *feats, q_hi, q_lo, seg_emb[:, None], query_emb[None, :], compat)


def per_device(acts, grads, proj_in, proj_out, queries, seg_emb, query_emb, compat, counts):
    segs_here = acts.shape[0]
    me = lax.axis_index("rank")
    grads_t = jnp.swapaxes(grads, 1, 2)
    w_in, w_out = proj_in.T, proj_out.T

    ids = lax.iota(jnp.int32, segs_here)
    before = (counts[None, :] > counts[:, None]) | (
        (counts[None, :] == counts[:, None]) & (ids[None, :] < ids[:, None])
    )
    place = jnp.sum(before.astype(jnp.int32), axis=1)

    def pick(positions, values):
        return jnp.sum(jnp.where(positions[:, None] == place[None, :], values[None, :], 0), axis=1)

    mine = jnp.asarray(PROJECT_POS)[me]
    segs, cnts = pick(mine, ids), pick(mine, counts)
    segs_gathered = pick(jnp.asarray(GATHER_POS)[me], ids)

    held = pick(jnp.asarray(OWNER_POS), counts).reshape(SLOTS, RANKS)
    need = jnp.max(up(held[0], 8) + up(held[1], 8) + up(held[2], 16))
    rung = jnp.sum((need > jnp.asarray(LADDER[:-1])).astype(jnp.int32))
    branches = [functools.partial(features, cap) for cap in LADDER]
    owned = lax.switch(rung, branches, segs, cnts, acts, grads_t, w_in, w_out)
    queries, owned = lax.optimization_barrier((queries, owned))
    q_hi, q_lo = halves(queries)
    line = jnp.concatenate([owned] + [hop(owned, shift(d, 0)) for d in (1, 2, 3)], axis=0)
    feats = [line] + [hop(line, shift(0, d)) for d in (1, 2, 3)]
    groups = lax.axis_size("dp")
    raw, sums = score(segs_gathered, feats, q_hi, q_lo, seg_emb, query_emb, compat)

    total = sums
    for core, z in ((1, 0), (0, 1), (0, 3)):
        other = [(i, (i // 2 ^ z) * 2 + (i % 2 ^ core)) for i in range(groups)]
        total = total + lax.ppermute(total, "dp", other)
    power = total[:1] / (segs_here * groups)
    return raw / jnp.sqrt(power + 1e-06)


def solution(mesh):
    return jax.shard_map(
        per_device,
        mesh=mesh,
        in_specs=(
            P("dp", None, "rank"),
            P("dp", None, "rank"),
            P("rank", None),
            P("rank", None),
            P("rank", None),
            P("dp"),
            P("rank"),
            P(),
            P("dp"),
        ),
        out_specs=P("dp", "rank"),
        check_vma=False,
    )
```

```python
import functools

import jax
import jax.numpy as jnp
import numpy as np
from jax import lax
from jax.experimental import pallas as pl
from jax.experimental.pallas import tpu as pltpu
from jax.sharding import PartitionSpec as P

SIDE = 4
RANKS = SIDE * SIDE
SLOTS = 3
BF16 = jnp.bfloat16
F32 = jnp.float32
LADDER = (544, 768)


def at(x, y):
    return (x % SIDE) * SIDE + y % SIDE


def home_x(rank):
    return sum(divmod(rank, SIDE)) % 2 == 0


def neighbour(home, flip, rank):
    x, y = divmod(rank, SIDE)
    return at(x ^ flip, y) if home == home_x(rank) else at(x, y ^ flip)


def stream_owner(home, stream, flip, rank):
    x, y = divmod(rank, SIDE)
    along_x = home == home_x(rank)
    via = neighbour(home, flip, rank)
    if along_x == home_x(via):
        return via if stream == 1 else second(3, via)
    return second(stream, via)


def second(kind, rank):
    x, y = divmod(rank, SIDE)
    even = (x + y) % 2 == 0
    if kind == 3:
        return at(x, y + 2) if even else at(x + 2, y)
    step = 1 if kind == 1 else -1
    return at(x + step, y) if even else at(x, y + step)


def destinations(rank):
    order = []
    for home, stream, flip in BLOCKS:
        order.append(stream_owner(home, stream, flip, rank))
    return order


BLOCKS = (
    [(True, 1, 1), (True, 1, 2), (False, 1, 1), (False, 1, 2)]
    + [(True, 2, 3), (True, 2, 2), (False, 2, 3), (False, 2, 2)]
    + [(True, 1, 3), (True, 2, 1), (False, 1, 3), (False, 2, 1)]
    + [(True, 1, 0), (True, 2, 0), (False, 1, 0), (False, 2, 0)]
)


def slot_positions(rank):
    zig = 7 - rank // 2 if rank % 2 == 0 else 15 - rank // 2
    sums = [r + (7 - r // 2 if r % 2 == 0 else 15 - r // 2) for r in range(RANKS)]
    above = sum(s > sums[rank] or (s == sums[rank] and r > rank) for r, s in enumerate(sums))
    return [rank, RANKS + zig, 2 * RANKS + above]


def gathered(rank):
    x, y = divmod(rank, SIDE)
    return [at(x - dx, y - dy) for dy in range(SIDE) for dx in range(SIDE)]


PROJECT_POS = np.array([sum((slot_positions(q) for q in destinations(r)), []) for r in range(RANKS)], np.int32)
GATHER_POS = np.array([sum((slot_positions(q) for q in gathered(r)), []) for r in range(RANKS)], np.int32)
OWNER_POS = np.array([slot_positions(q) for q in range(RANKS)], np.int32).T.reshape(-1)
FLIPS = {
    (home, flip): [(r, neighbour(home, flip, r)) for r in range(RANKS)] for home in (True, False) for flip in (1, 3)
}
SECOND = {kind: [(r, second(kind, r)) for r in range(RANKS)] for kind in (1, 2, 3)}


def shift(dx, dy):
    return [(r, at(r // SIDE + dx, r % SIDE + dy)) for r in range(RANKS)]


def up(n, m):
    return (n + (m - 1)) // m * m


def project_kernel(first, plans, acts, grads, w_in, w_out, *refs):
    outs, (act_buf, grad_buf, made_buf, spill, sems, out_sems) = refs[:4], refs[4:]
    toks = act_buf.shape[1]
    cap = outs[0].shape[0] // 2

    def copies(j):
        s = plans[0, first + j]
        return (
            pltpu.make_async_copy(acts.at[s], act_buf.at[j], sems.at[j, 0]),
            pltpu.make_async_copy(grads.at[s], grad_buf.at[j], sems.at[j, 1]),
        )

    for j in range(act_buf.shape[0]):
        for copy in copies(j):
            copy.start()
    w_a = jnp.concatenate([jnp.zeros_like(w_in[...]), w_in[...]], axis=0)
    nt = (((1,), (1,)), ((), ()))

    def rows(j):
        side_g = jnp.dot(w_out[...], grad_buf[j], preferred_element_type=F32)
        side_a = lax.dot_general(act_buf[j], w_a, nt, preferred_element_type=F32)
        return side_a + jnp.concatenate([side_g, jnp.zeros_like(side_g)], axis=0).T

    leaving = []
    for h in range(len(outs)):
        out = made_buf.at[h]

        def block(i, _):
            j = (h * 2 + i) * SLOTS
            for k in range(SLOTS):
                for copy in copies(j + k):
                    copy.wait()
            made = [rows(j + k) for k in range(SLOTS)]
            base = pl.multiple_of(i * cap, 8)
            mid = pl.multiple_of(base + up(plans[1, first + j], 8), 8)
            last = pl.multiple_of(mid + up(plans[1, first + j + 1], 8), 8)
            out[pl.ds(base, toks), :] = made[0]
            out[pl.ds(mid, toks), :] = made[1]
            spill[...] = made[2]

            def piece(n, _):
                to = pl.multiple_of(last + n * 16, 8)
                out[pl.ds(to, 16), :] = spill[pl.ds(pl.multiple_of(n * 16, 16), 16), :]
                return 0

            return lax.fori_loop(0, up(plans[1, first + j + 2], 16) // 16, piece, 0)

        lax.fori_loop(0, 2, block, 0)
        leaving.append(pltpu.make_async_copy(out.at[pl.ds(0, 2 * cap)], outs[h], out_sems.at[h]))
        leaving[-1].start()
    for copy in leaving:
        copy.wait()


def project(part, cap, plans, acts, grads_t, w_in, w_out):
    toks, fa = acts.shape[1:]
    fg = grads_t.shape[1]
    n = acts.shape[0] // 2
    vmem = pl.BlockSpec(memory_space=pltpu.VMEM)
    smem = pl.BlockSpec(memory_space=pltpu.SMEM)
    any_ = pl.BlockSpec(memory_space=pl.ANY)
    return pl.pallas_call(
        functools.partial(project_kernel, part * n),
        in_specs=[smem, any_, any_, vmem, vmem],
        out_specs=[any_] * 4,
        out_shape=[jax.ShapeDtypeStruct((2 * cap, 128), F32)] * 4,
        scratch_shapes=[
            pltpu.VMEM((n, toks, fa), BF16),
            pltpu.VMEM((n, fg, toks), BF16),
            pltpu.VMEM((4, 2 * cap + 8, 128), F32),
            pltpu.VMEM((toks, 128), F32),
            pltpu.SemaphoreType.DMA((n, 2)),
            pltpu.SemaphoreType.DMA((4,)),
        ],
        compiler_params=pltpu.CompilerParams(vmem_limit_bytes=40 * 2**20),
        cost_estimate=pl.CostEstimate(
            flops=n * toks * 2 * 64 * (fa + fg),
            bytes_accessed=n * toks * 2 * (fa + fg) + 8 * cap * 512,
            transcendentals=0,
        ),
        name="project",
    )(plans, acts, grads_t, w_in, w_out)


def split(x):
    hi = x.astype(BF16)
    return hi, (x - hi.astype(F32)).astype(BF16)


def outer_kernel(at, plans, own, r1, r2, r3, out, pair):
    cnts = [plans[1, at + k] for k in range(SLOTS)]
    total = (own[...] + r1[...]) + (r2[...] + r3[...])
    cap = total.shape[0]
    row = lax.broadcasted_iota(jnp.int32, (cap, 128), 0)
    off1 = up(cnts[0], 8)
    off2 = off1 + up(cnts[1], 8)
    live = [
        row < cnts[0],
        (row >= off1) & (row < off1 + cnts[1]),
        (row >= off2) & (row < off2 + cnts[2]),
    ]
    total = jnp.where(live[0] | live[1] | live[2], total, 0.0)
    lane = lax.broadcasted_iota(jnp.int32, (cap, 128), 1)
    act = jnp.where(lane < 64, pltpu.roll(total, 64, 1), total)
    a_hi, a_lo = split(act)
    total_t = total.T[:64]
    col = lax.broadcasted_iota(jnp.int32, (64, cap), 1)
    live_t = [
        col < cnts[0],
        (col >= off1) & (col < off1 + cnts[1]),
        (col >= off2) & (col < off2 + cnts[2]),
    ]
    grad = jnp.concatenate([jnp.where(m, total_t, 0.0) for m in live_t], axis=0)
    g_hi, g_lo = split(grad)
    dot = functools.partial(jnp.dot, preferred_element_type=F32)
    pair[...] = dot(g_hi, a_hi) + (dot(g_hi, a_lo) + dot(g_lo, a_hi))
    first = pair[pl.ds(0, 96, stride=2), :]
    other = pair[pl.ds(1, 96, stride=2), :]
    lane = lax.broadcasted_iota(jnp.int32, (96, 128), 1)
    out[...] = jnp.where(lane < 64, first, other)


def outer(at, plans, parts):
    cap = parts[0].shape[0]
    spec = pl.BlockSpec(memory_space=pltpu.VMEM)
    return pl.pallas_call(
        functools.partial(outer_kernel, at),
        in_specs=[pl.BlockSpec(memory_space=pltpu.SMEM)] + [spec] * 4,
        out_specs=spec,
        out_shape=jax.ShapeDtypeStruct((SLOTS * 32, 128), F32),
        scratch_shapes=[pltpu.VMEM((SLOTS * 64, 128), F32)],
        compiler_params=pltpu.CompilerParams(vmem_limit_bytes=24 * 2**20),
        cost_estimate=pl.CostEstimate(flops=6 * 192 * cap * 128, bytes_accessed=4 * cap * 512, transcendentals=0),
        name="outer",
    )(plans, *parts)


def hop(x, pairs):
    return lax.ppermute(x, "rank", pairs)


def features(cap, plans, acts, grads_t, w_in, w_out):
    made = [project(part, cap, plans, acts, grads_t, w_in, w_out) for part in range(2)]
    made = [made[0][:2], made[0][2:], made[1][:2], made[1][2:]]
    flip = {1: 1, 2: 3}
    orders = [(stream, home) for stream in (1, 2) for home in (True, False)]
    got, onward, done = {}, {}, {}
    for stream, home in orders:
        got[not home, stream] = hop(made[stream - 1][0 if home else 1], FLIPS[home, flip[stream]])
    came = {}
    for stream, home in orders:
        at_b = made[2][0 if home else 1][(stream - 1) * cap : stream * cap]
        onward[home, stream] = at_b + got[home, stream][cap:]
        came[not home, stream] = hop(onward[home, stream], FLIPS[home, flip[3 - stream]])
    came[True, 1], came[False, 1], _, _ = lax.optimization_barrier(
        (came[True, 1], came[False, 1], onward[True, 2], onward[False, 2])
    )
    for stream, home in orders:
        stay = made[3][0 if home else 1][(stream - 1) * cap : stream * cap]
        done[home, stream] = (stay + got[home, stream][:cap]) + came[home, stream]
    parts = [
        done[True, 1],
        hop(done[False, 1], SECOND[1]),
        hop(done[False, 2], SECOND[2]),
        hop(done[True, 2], SECOND[3]),
    ]
    return outer(BLOCKS.index((True, 1, 0)) * SLOTS, plans, parts)


def halves_kernel(queries, hi, lo):
    hi[...], lo[...] = split(queries[...])


def halves(queries):
    nq, nf = queries.shape
    steps = 4
    spec = pl.BlockSpec((nq // steps, nf), lambda i: (i, 0))
    out = jax.ShapeDtypeStruct((nq, nf), BF16)
    return pl.pallas_call(
        halves_kernel,
        grid=(steps,),
        in_specs=[spec],
        out_specs=[spec, spec],
        out_shape=[out, out],
        compiler_params=pltpu.CompilerParams(vmem_limit_bytes=48 * 2**20),
        cost_estimate=pl.CostEstimate(flops=nq * nf * 2, bytes_accessed=nq * nf * 8, transcendentals=0),
        name="halves",
    )(queries)


def score_kernel(plans, *refs):
    feats, (q_hi, q_lo, seg_kind, query_kind, compat, raw_out, sums_out, placed) = refs[:4], refs[4:]
    n = placed.shape[0]
    nt = (((1,), (1,)), ((), ()))
    dot = functools.partial(lax.dot_general, dimension_numbers=nt, preferred_element_type=F32)
    width = q_hi.shape[1] // 128
    total = jnp.zeros(placed.shape, F32)
    for m in range(0, width, 2):
        left = jnp.concatenate(
            [
                jnp.concatenate([f[pl.ds(m + e, f.shape[0] // width, stride=width), :] for f in feats], axis=0)
                for e in range(2)
            ],
            axis=1,
        )
        l_hi, l_lo = split(left)
        cols = slice(m * 128, (m + 2) * 128)
        both = dot(jnp.concatenate([l_hi, l_lo], axis=0), q_hi[:, cols])
        total = total + ((both[:n] + both[n:]) + dot(l_hi, q_lo[:, cols]))
    placed[...] = total
    for slot in range(n):
        raw_out[pl.ds(plans[2, slot], 1), :] = placed[slot : slot + 1, :]
    kinds = compat.shape[0]
    one_seg = (seg_kind[...] == lax.broadcasted_iota(jnp.int32, (n, kinds), 1)).astype(F32)
    nq = query_kind.shape[1]
    one_query = (query_kind[...] == lax.broadcasted_iota(jnp.int32, (kinds, nq), 0)).astype(F32)
    table = jnp.dot(one_seg, compat[...].astype(F32), preferred_element_type=F32)
    allowed = jnp.dot(table, one_query, preferred_element_type=F32)
    raw = raw_out[...] * allowed
    raw_out[...] = raw
    sums_out[...] = jnp.broadcast_to(jnp.sum(raw * raw, axis=0, keepdims=True), sums_out.shape)


def score(plans, feats, q_hi, q_lo, seg_emb, query_emb, compat):
    n, (nq, nf) = seg_emb.shape[0], q_hi.shape
    vmem = pl.BlockSpec(memory_space=pltpu.VMEM)
    return pl.pallas_call(
        score_kernel,
        in_specs=[pl.BlockSpec(memory_space=pltpu.SMEM)] + [vmem] * 9,
        out_specs=[vmem, vmem],
        out_shape=(jax.ShapeDtypeStruct((n, nq), F32), jax.ShapeDtypeStruct((8, nq), F32)),
        scratch_shapes=[pltpu.VMEM((n, nq), F32)],
        compiler_params=pltpu.CompilerParams(vmem_limit_bytes=24 * 2**20),
        cost_estimate=pl.CostEstimate(flops=6 * n * nq * nf, bytes_accessed=nq * nf * 4, transcendentals=0),
        name="score",
    )(plans, *feats, q_hi, q_lo, seg_emb[:, None], query_emb[None, :], compat)


def plan_kernel(me, counts, positions, out):
    n = counts.shape[1]
    wide = 128
    row = jnp.concatenate([counts[...], jnp.full((1, wide - n), -1, jnp.int32)], axis=1)
    c_row = jnp.broadcast_to(row, (wide, wide)).astype(F32)
    c_col = c_row.T
    id_row = lax.broadcasted_iota(jnp.int32, (wide, wide), 1)
    id_col = lax.broadcasted_iota(jnp.int32, (wide, wide), 0)
    before = (c_row > c_col) | ((c_row == c_col) & (id_row < id_col))
    place = jnp.sum(before.astype(jnp.int32), axis=1, keepdims=True)

    def pick(where, values):
        return jnp.sum(jnp.where(place == where, values, 0), axis=0, keepdims=True)

    counts_col = c_col.astype(jnp.int32)
    mine = positions[pl.ds(me[0], 1), :]
    segs, cnts = pick(mine, id_col), pick(mine, counts_col)
    back = pick(positions[pl.ds(me[0] + RANKS, 1), :], id_col)
    held = [pick(positions[pl.ds(2 * RANKS + k, 1), :], counts_col) for k in range(SLOTS)]
    load = sum(up(h, 8) for h in held)
    need = jnp.broadcast_to(jnp.max(load, axis=1, keepdims=True), (1, wide))
    rung = sum((need > cap).astype(jnp.int32) for cap in LADDER[:-1])
    out[...] = jnp.concatenate([segs, cnts, back, rung] + [rung] * 4, axis=0)


def plan(me, counts):
    n = counts.shape[0]
    table = np.full((40, 128), 127, np.int32)
    table[:RANKS, :n] = PROJECT_POS
    table[RANKS : 2 * RANKS, :n] = GATHER_POS
    table[2 * RANKS : 2 * RANKS + SLOTS, :RANKS] = OWNER_POS.reshape(SLOTS, RANKS)
    vmem = pl.BlockSpec(memory_space=pltpu.VMEM)
    return pl.pallas_call(
        plan_kernel,
        in_specs=[pl.BlockSpec(memory_space=pltpu.SMEM), vmem, vmem],
        out_specs=vmem,
        out_shape=jax.ShapeDtypeStruct((8, 128), jnp.int32),
        name="plan",
    )(me[None], counts[None, :], jnp.asarray(table))


def per_device(acts, grads, proj_in, proj_out, queries, seg_emb, query_emb, compat, counts):
    segs_here = acts.shape[0]
    me = lax.axis_index("rank")
    grads_t = jnp.swapaxes(grads, 1, 2)
    w_in, w_out = proj_in.T, proj_out.T

    plans = plan(me, counts)
    rung = plans[3, 0]
    branches = [functools.partial(features, cap) for cap in LADDER]
    owned = lax.switch(rung, branches, plans, acts, grads_t, w_in, w_out)
    queries, owned = lax.optimization_barrier((queries, owned))
    q_hi, q_lo = halves(queries)
    line = jnp.concatenate([owned] + [hop(owned, shift(d, 0)) for d in (1, 2, 3)], axis=0)
    feats = [line] + [hop(line, shift(0, d)) for d in (1, 2, 3)]
    groups = lax.axis_size("dp")
    raw, sums = score(plans, feats, q_hi, q_lo, seg_emb, query_emb, compat)

    total = sums
    for core, z in ((1, 0), (0, 1), (0, 3)):
        other = [(i, (i // 2 ^ z) * 2 + (i % 2 ^ core)) for i in range(groups)]
        total = total + lax.ppermute(total, "dp", other)
    power = total[:1] / (segs_here * groups)
    return raw / jnp.sqrt(power + 1e-06)


def solution(mesh):
    return jax.shard_map(
        per_device,
        mesh=mesh,
        in_specs=(
            P("dp", None, "rank"),
            P("dp", None, "rank"),
            P("rank", None),
            P("rank", None),
            P("rank", None),
            P("dp"),
            P("rank"),
            P(),
            P("dp"),
        ),
        out_specs=P("dp", "rank"),
        check_vma=False,
    )
```
